256 devices in a mesh: aux: 4 (over x), row: 16 (over z_hi, y), col: 4 (over z_lo, core).
Axes of the slice: x: 4, y: 4, z: 8 (z_hi: 4, z_lo: 2; z = z_hi * 2 + z_lo), core: 2. Of those that a mesh axis runs over, the one named last changes fastest.
Arguments:
- factors: bfloat16 [8, 4, 2560, 10240], P('aux', None, 'row', 'col'), may hold values from -0.078125 to 0.078125
- orbitals: bfloat16 [10240, 512], P('col'), may hold values from -0.25 to 0.25
- tile_mask: int32 [8, 80, 80], P('aux'), may hold values from 0 to 1, as said below
Outputs:
- exchange: float32 [10240, 10240], P(('aux', 'row'), 'col')
The draws below stay inside these ranges and needn't reach their ends.
Inputs may be any that keep to these rules, and one draw needn't show every extreme that they name: `tile_mask`: 0 or 1; present tiles cluster around a centre tile drawn for each auxiliary function, and absent tiles occur everywhere.
All inputs are finite; a program needn't handle non-finite values.
Results may differ from the reference program's by a relative error of at most 0.02.
Values may be sent and summed in bfloat16 or wider, within the bound.
A program may use at most 64 MiB of HBM per device.

```python
import jax
import jax.numpy as jnp
from jax import lax

NB = 10240
NOCC = 512
TILE = 128
QDEV = 2
QAUX = 8
N_AUX = 4
N_COL = 4


def draw_tile_mask(key, part):
    tile_count = NB // TILE
    first_key, second_key = jax.random.split(key)
    centres = jax.random.randint(first_key, (QAUX, 1, 1), 0, tile_count)
    row_ids = jnp.arange(tile_count, dtype=jnp.int32)[None, :, None]
    col_ids = jnp.arange(tile_count, dtype=jnp.int32)[None, None, :]
    distance = jnp.abs(row_ids - centres) + jnp.abs(col_ids - centres)
    percent = 20 + 70 * jnp.maximum(0, tile_count - 2 * distance) // tile_count
    rolled = jax.random.randint(second_key, (QAUX, tile_count, tile_count), 0, 100)
    return (rolled < percent).astype(jnp.int32)


def block_levels(rng, extent, cuts, low, largest):
    factor_of = 1.0
    for axis_at, parts in cuts:
        heights = jax.random.uniform(jax.random.fold_in(jax.random.fold_in(rng, 6), axis_at), (parts,), jnp.float32, low / len(cuts), largest / len(cuts))
        factor_of = factor_of * jnp.repeat(jnp.exp(heights), extent[axis_at] // parts).reshape((-1,) + (1,) * (len(extent) - 1 - axis_at))
    return factor_of


def scatter_about(rng, extent, deviation, bound, shards=(), kind=jnp.bfloat16):
    factor_of = block_levels(rng, extent, shards, -0.22, 0.18) if shards else 1.0
    drawn = jax.random.normal(rng, extent, jnp.float32) * deviation * factor_of
    return jnp.minimum(jnp.maximum(drawn, -bound), bound).astype(kind)


def setup_inputs(seed: int = 0) -> dict:
    keys = jax.random.split(jax.random.key(seed), 4)
    return {
        "factors": scatter_about(keys[0], (QAUX, N_AUX, NB // N_AUX, NB), (NB // 2) ** -0.5, 0.078125, ((0, 4), (2, 16), (3, 4))),
        "orbitals": scatter_about(keys[1], (NB, NOCC), NOCC ** -0.5, 0.25, ((0, 4),)),
        "tile_mask": draw_tile_mask(jax.random.fold_in(keys[3], 71), 0),
    }


def masked_product(factor, tile_flags, orbitals):
    tile_count = NB // TILE
    masked = factor.reshape(tile_count, TILE, tile_count, TILE) * tile_flags.astype(jnp.bfloat16)[:, None, :, None]
    masked = masked.reshape(NB, NB)
    col_width = NB // N_COL
    summed = jnp.zeros((NB, NOCC), jnp.float32)
    for quarter in range(N_COL):
        partial_term = jnp.dot(masked[:, quarter * col_width:(quarter + 1) * col_width],
                               orbitals[quarter * col_width:(quarter + 1) * col_width],
                               preferred_element_type=jnp.float32)
        summed = summed + partial_term.astype(jnp.bfloat16).astype(jnp.float32)
    return summed.astype(jnp.bfloat16)


def reference(factors, orbitals, tile_mask):
    flat_factors = factors.reshape(QAUX, NB, NB)
    orbital_rows = lax.map(lambda operands: masked_product(operands[0], operands[1], orbitals), (flat_factors, tile_mask))
    result = jnp.zeros((NB, NB), jnp.float32)
    for group_index in range(N_AUX):
        panel = orbital_rows[group_index * QDEV:(group_index + 1) * QDEV].astype(jnp.float32)
        partial_k = jnp.einsum("qik,qjk->ij", panel, panel, precision=lax.Precision.HIGHEST)
        result = result + partial_k.astype(jnp.bfloat16).astype(jnp.float32)
    return result
```

```python
import jax
import jax.numpy as jnp
from jax import lax
from jax.experimental import pallas as pl
from jax.experimental.pallas import tpu as pltpu
from jax.sharding import PartitionSpec as P

NB = 10240
TILE = 128
MESH = pl.DeviceIdType.MESH
BF = jnp.bfloat16
F32 = jnp.float32
NT = (((1,), (1,)), ((), ()))
NX, NY, NZ = 4, 4, 4
ROWS, HALF, OCC = 160, 80, 512
WIDE = NY * ROWS
COLS = NB // 4
LAYERS = (0, 1, 3, 2)
N_SEMS = 80


def kernel(mask_ref, factors_ref, orbitals_ref, out_ref,
           fbuf, cbuf, mexp, masked, give, keep, got_a, put_b, got_b, panels, left, prod,
           far, near, got_far, got_near, held, in_sem, send_sem, recv_sem):
    x = lax.axis_index("aux")
    row = lax.axis_index("row")
    col = lax.axis_index("col")
    zh, y = lax.div(row, NY), lax.rem(row, NY)
    core_col = col + 1 - 2 * lax.rem(col, 2)
    pair_col = lax.rem(col + 2, 4)
    cross_col = 3 - col

    def at_x(d):
        return lax.rem(x + d + NX, NX)

    def at_y(d):
        return lax.rem(y + d + NY, NY)

    def at_z(d):
        return lax.rem(zh + d + NZ, NZ)

    core = {"col": core_col}
    pair = {"col": pair_col}
    y_dev = {d: {"row": zh * NY + at_y(d)} for d in (1, -1)}
    z_dev = {d: {"row": at_z(d) * NY + y} for d in (1, -1)}
    x_dev = {d: {"aux": at_x(d)} for d in (1, -1)}

    barrier = pltpu.get_barrier_semaphore()
    partners = [core, pair, y_dev[1], y_dev[-1], z_dev[1], z_dev[-1], x_dev[1], x_dev[-1]]
    for partner in partners:
        pl.semaphore_signal(barrier, inc=1, device_id=partner, device_id_type=MESH)

    order = (cross_col, pair_col, core_col, col)
    loads = {}
    load = pltpu.make_async_copy(orbitals_ref, cbuf, in_sem.at[8])
    load.start()
    for n, (q, s) in enumerate(((0, 0), (0, 1), (1, 0), (1, 1), (0, 2), (0, 3), (1, 2), (1, 3))):
        piece = pltpu.make_async_copy(factors_ref.at[q, order[s]], fbuf.at[q, order[s]], in_sem.at[n])
        piece.start()
        loads[q, s] = piece

    pick_row = lax.broadcasted_iota(jnp.int32, (64, 80), 0)
    pick_col = lax.broadcasted_iota(jnp.int32, (64, 80), 1)
    tile_row = (pick_row // 16) * (COLS // TILE) + (row * (ROWS // 32) + pick_row % 8) // (TILE // 32)
    spread_row = lax.broadcasted_iota(jnp.int32, (80, COLS), 0)
    spread_col = lax.broadcasted_iota(jnp.int32, (80, COLS), 1)
    spread = (spread_row == col * (COLS // TILE) + spread_col // TILE).astype(BF)
    flags = jnp.zeros((64, 80), F32)
    for q in range(2):
        pick = ((pick_col == tile_row) & ((pick_row % 16) // 8 == q)).astype(BF)
        flags = flags + jnp.dot(pick, mask_ref[q].astype(F32).astype(BF), preferred_element_type=F32)
    mexp[...] = jnp.dot(flags.astype(BF), spread, preferred_element_type=F32).reshape(4, 16, COLS)

    sends = []
    used = [0]

    def sem():
        used[0] += 1
        return used[0] - 1

    def send(src, dst, index, to):
        copy = pltpu.make_async_remote_copy(
            src_ref=src, dst_ref=dst, send_sem=send_sem.at[index], recv_sem=recv_sem.at[index],
            device_id=to, device_id_type=MESH)
        copy.start()
        sends.append(copy)

    def arrived(dst, index, to):
        pltpu.make_async_remote_copy(
            src_ref=dst, dst_ref=dst, send_sem=send_sem.at[index], recv_sem=recv_sem.at[index],
            device_id=to, device_id_type=MESH).wait_recv()

    s_a = {(q, s): sem() for q in range(2) for s in range(2)}
    s_b = {q: sem() for q in range(2)}
    s_pair = {q: sem() for q in range(2)}
    s_core = {q: sem() for q in range(2)}
    s_cross = {q: sem() for q in range(2)}
    s_z1 = {(q, d): sem() for q in range(2) for d in (1, -1)}
    s_z2 = {(q, d): sem() for q in range(2) for d in (1, -1)}
    s_y1 = {(n, q, d): sem() for n in range(NZ) for q in range(2) for d in (1, -1)}
    s_y2 = {(n, q, d): sem() for n in range(NZ) for q in range(2) for d in (1, -1)}
    s_far = {(i, d): sem() for i in range(NZ) for d in (1, -1)}
    s_near = {(i, d, h): sem() for i in range(NZ) for d in (1, -1) for h in range(2)}

    def partial_product(q, s):
        quarter = order[s]
        loads[q, s].wait()
        for g in range(ROWS // 32):
            flag_row = mexp[quarter, pl.ds(8 * q + g, 1), :].astype(BF)
            masked[pl.ds(32 * g, 32), :] = fbuf[q, quarter, pl.ds(32 * g, 32), :] * flag_row
        return jnp.dot(masked[...], cbuf[...], preferred_element_type=F32)

    def give_core(q, n):
        give[q, n] = partial_product(q, 2 * n).astype(BF)
        send(give.at[q, n], got_a.at[q, n], s_a[q, n], core)

    def give_pair(q):
        arrived(got_a.at[q, 0], s_a[q, 0], core)
        put_b[q] = (keep[q, 0] + got_a[q, 0].astype(F32)).astype(BF)
        send(put_b.at[q], got_b.at[q], s_b[q], pair)

    def finish_rows(q):
        arrived(got_a.at[q, 1], s_a[q, 1], core)
        arrived(got_b.at[q], s_b[q], pair)
        rows = (keep[q, 1] + got_a[q, 1].astype(F32) + got_b[q].astype(F32)).astype(BF)
        panels[zh, q, y] = rows
        left[q, col] = rows
        own = panels.at[zh, q, y]
        send(left.at[q, col], left.at[q, col], s_pair[q], pair)
        for d in (1, -1):
            send(own, own, s_y1[0, q, d], y_dev[d])
        for d in (1, -1):
            send(own, own, s_z1[q, d], z_dev[d])
        send(left.at[q, col], left.at[q, col], s_core[q], core)

    load.wait()
    give_value = partial_product(0, 0).astype(BF)
    give[0, 0] = give_value
    pl.semaphore_wait(barrier, len(partners))
    send(give.at[0, 0], got_a.at[0, 0], s_a[0, 0], core)
    keep[0, 0] = partial_product(0, 1)
    give_core(1, 0)
    give_pair(0)
    keep[1, 0] = partial_product(1, 1)
    give_core(0, 1)
    give_pair(1)
    keep[0, 1] = partial_product(0, 3)
    give_core(1, 1)
    keep[1, 1] = partial_product(1, 3)

    halves = {1: pl.ds(0, HALF), -1: pl.ds(HALF, HALF)}

    def along_y1(n, q):
        own = panels.at[at_z(LAYERS[n]), q, y]
        for d in (1, -1):
            send(own, own, s_y1[n, q, d], y_dev[d])

    def along_y2(n, q):
        for d in (1, -1):
            block = panels.at[at_z(LAYERS[n]), q, at_y(-d)]
            arrived(block, s_y1[n, q, d], y_dev[-d])
            part = panels.at[at_z(LAYERS[n]), q, at_y(-d), halves[d]]
            send(part, part, s_y2[n, q, d], y_dev[d])

    def along_z2(q):
        for d in (1, -1):
            block = panels.at[at_z(-d), q, y]
            arrived(block, s_z1[q, d], z_dev[-d])
            part = panels.at[at_z(-d), q, y, halves[d]]
            send(part, part, s_z2[q, d], z_dev[d])

    def end_z(q):
        for d in (1, -1):
            arrived(panels.at[at_z(2), q, y, halves[d]], s_z2[q, d], z_dev[-d])

    def pass_cross(q):
        arrived(left.at[q, pair_col], s_pair[q], pair)
        send(left.at[q, pair_col], left.at[q, pair_col], s_cross[q], core)

    def end_y(n):
        for q in range(2):
            for d in (1, -1):
                arrived(panels.at[at_z(LAYERS[n]), q, at_y(2), halves[d]], s_y2[n, q, d], y_dev[-d])

    def end_left():
        for q in range(2):
            arrived(left.at[q, core_col], s_core[q], core)
            arrived(left.at[q, cross_col], s_cross[q], core)

    def product(n):
        layer = at_z(LAYERS[n])
        value = jnp.zeros((4 * ROWS, WIDE), F32)
        for q in range(2):
            value = value + lax.dot_general(
                left[q].reshape(4 * ROWS, OCC), panels[layer, q].reshape(WIDE, OCC), NT,
                preferred_element_type=F32)
        prod[...] = value.reshape(4, ROWS, WIDE)
        far[n] = prod[at_x(2)].astype(BF)
        for d in (1, -1):
            send(far.at[n, halves[d]], got_far.at[n, 0 if d == 1 else 1], s_far[n, d], x_dev[d])
        for d in (1, -1):
            slot = 0 if d == 1 else 1
            mine, other = halves[d], halves[-d]
            near[n, slot, other] = prod[at_x(d), other].astype(BF)
            held[n, slot] = prod[at_x(d), mine]
            send(near.at[n, slot, other], got_near.at[n, slot, other], s_near[n, d, 1], x_dev[d])
        out_ref[layer] = prod[x]

    def pass_on(n):
        for d in (1, -1):
            slot = 0 if d == 1 else 1
            mine = halves[d]
            arrived(got_far.at[n, slot], s_far[n, d], x_dev[-d])
            near[n, slot, mine] = (held[n, slot] + got_far[n, slot].astype(F32)).astype(BF)
            send(near.at[n, slot, mine], got_near.at[n, slot, mine], s_near[n, d, 0], x_dev[d])

    def finish(n):
        layer = at_z(LAYERS[n])
        for d in (1, -1):
            slot = 0 if d == 1 else 1
            arrived(got_near.at[n, slot, halves[d]], s_near[n, d, 0], x_dev[-d])
            arrived(got_near.at[n, slot, halves[-d]], s_near[n, d, 1], x_dev[-d])
        out_ref[layer] += got_near[n, 0].astype(F32) + got_near[n, 1].astype(F32)

    finish_rows(0)
    finish_rows(1)
    along_y2(0, 0)
    along_y2(0, 1)
    pass_cross(0)
    along_z2(0)
    along_y1(1, 0)
    along_y1(2, 0)
    pass_cross(1)
    end_left()
    end_y(0)
    product(0)
    along_z2(1)
    along_y1(1, 1)
    along_y1(2, 1)
    pass_on(0)
    along_y2(1, 0)
    along_y2(2, 0)
    end_z(0)
    along_y1(3, 0)
    along_y2(1, 1)
    along_y2(2, 1)
    end_z(1)
    along_y1(3, 1)
    finish(0)
    end_y(1)
    product(1)
    end_y(2)
    product(2)
    along_y2(3, 0)
    pass_on(1)
    pass_on(2)
    along_y2(3, 1)
    finish(1)
    finish(2)
    end_y(3)
    product(3)
    pass_on(3)
    finish(3)
    for copy in sends:
        copy.wait_send()


def on_device(factors, orbitals, tile_mask):
    vmem = pl.BlockSpec(memory_space=pltpu.VMEM)
    hbm = pl.BlockSpec(memory_space=pl.ANY)
    out = pl.pallas_call(
        kernel,
        out_shape=jax.ShapeDtypeStruct((NZ, ROWS, WIDE), F32),
        in_specs=[vmem, hbm, hbm],
        out_specs=vmem,
        scratch_shapes=[
            pltpu.VMEM((2, 4, ROWS, COLS), BF),
            pltpu.VMEM((COLS, OCC), BF),
            pltpu.VMEM((4, 16, COLS), F32),
            pltpu.VMEM((ROWS, COLS), BF),
            pltpu.VMEM((2, 2, ROWS, OCC), BF),
            pltpu.VMEM((2, 2, ROWS, OCC), F32),
            pltpu.VMEM((2, 2, ROWS, OCC), BF),
            pltpu.VMEM((2, ROWS, OCC), BF),
            pltpu.VMEM((2, ROWS, OCC), BF),
            pltpu.VMEM((NZ, 2, NY, ROWS, OCC), BF),
            pltpu.VMEM((2, 4, ROWS, OCC), BF),
            pltpu.VMEM((4, ROWS, WIDE), F32),
            pltpu.VMEM((NZ, ROWS, WIDE), BF),
            pltpu.VMEM((NZ, 2, ROWS, WIDE), BF),
            pltpu.VMEM((NZ, 2, HALF, WIDE), BF),
            pltpu.VMEM((NZ, 2, ROWS, WIDE), BF),
            pltpu.VMEM((NZ, 2, HALF, WIDE), F32),
            pltpu.SemaphoreType.DMA((9,)),
            pltpu.SemaphoreType.DMA((N_SEMS,)),
            pltpu.SemaphoreType.DMA((N_SEMS,)),
        ],
        compiler_params=pltpu.CompilerParams(
            collective_id=0, has_side_effects=True, vmem_limit_bytes=56 * 2**20),
        cost_estimate=pl.CostEstimate(flops=7 * 10**9, bytes_accessed=12 * 10**6, transcendentals=0),
        name="exchange",
    )(tile_mask, factors, orbitals)
    return out.transpose(1, 0, 2).reshape(ROWS, NZ * WIDE)


def solution(mesh):
    placed = (P("aux", None, "row", "col"), P("col", None), P("aux", None, None))
    return jax.shard_map(
        on_device, mesh=mesh, in_specs=placed, out_specs=P(("aux", "row"), "col"), check_vma=False
    )
```

```python
import jax
import jax.numpy as jnp
from jax import lax
from jax.experimental import pallas as pl
from jax.experimental.pallas import tpu as pltpu
from jax.sharding import PartitionSpec as P

NB = 10240
TILE = 128
MESH = pl.DeviceIdType.MESH
BF = jnp.bfloat16
F32 = jnp.float32
NT = (((1,), (1,)), ((), ()))
NX, NY, NZ = 4, 4, 4
ROWS, HALF, OCC = 160, 80, 512
WIDE = NY * ROWS
COLS = NB // 4
PARTS = 4
PART = 2 * OCC // PARTS
Y_FIRST = (3,)
CUT = 384
SPLIT = (2, 3)
N_SEMS = 12 + 23 * PARTS + 6 * len(Y_FIRST) + 24 + 6 * len(SPLIT)


def kernel(mask_hbm, factors_ref, orbitals_ref, out_ref,
           fbuf, cbuf, mask_ref, mexp, masked, give, keep, got_a, put_b, got_b, panels, left, prod, turned, natural, gathered,
           far, near, got_far, got_near, held, in_sem, send_sem, recv_sem):
    x = lax.axis_index("aux")
    row = lax.axis_index("row")
    col = lax.axis_index("col")
    zh, y = lax.div(row, NY), lax.rem(row, NY)
    core_col = col + 1 - 2 * lax.rem(col, 2)
    pair_col = lax.rem(col + 2, 4)
    cross_col = 3 - col

    def at_x(d):
        return lax.rem(x + d + NX, NX)

    def at_y(d):
        return lax.rem(y + d + NY, NY)

    def at_z(d):
        return lax.rem(zh + d + NZ, NZ)

    side = 2 * lax.div(col, 2) - 1
    core = {"col": core_col}
    pair = {"col": pair_col}
    next_chip = {"row": at_z(side) * NY + y, "col": pair_col}
    y_dev = {d: {"row": zh * NY + at_y(d)} for d in (1, -1)}
    z_near, z_far = {"row": at_z(side) * NY + y}, {"row": at_z(-side) * NY + y}
    x_dev = {d: {"aux": at_x(d)} for d in (1, -1)}
    layers = (zh, at_z(side), at_z(-side), at_z(2))

    barrier = pltpu.get_barrier_semaphore()
    partners = [core, pair, next_chip, y_dev[1], y_dev[-1], z_near, z_far, x_dev[1], x_dev[-1]]
    for partner in partners:
        pl.semaphore_signal(barrier, inc=1, device_id=partner, device_id_type=MESH)

    order = (core_col, col, cross_col, pair_col)
    flags_in = pltpu.make_async_copy(mask_hbm, mask_ref, in_sem.at[9])
    flags_in.start()
    loads = {}
    load = pltpu.make_async_copy(orbitals_ref, cbuf, in_sem.at[8])
    load.start()
    for n, (q, s) in enumerate(((0, 0), (0, 1), (1, 0), (1, 1), (0, 2), (0, 3), (1, 2), (1, 3))):
        piece = pltpu.make_async_copy(factors_ref.at[q, order[s]], fbuf.at[q, order[s]], in_sem.at[n])
        piece.start()
        loads[q, s] = piece

    flags_in.wait()
    pick_row = lax.broadcasted_iota(jnp.int32, (64, 80), 0)
    pick_col = lax.broadcasted_iota(jnp.int32, (64, 80), 1)
    tile_row = (pick_row // 16) * (COLS // TILE) + (row * (ROWS // 32) + pick_row % 8) // (TILE // 32)
    spread_row = lax.broadcasted_iota(jnp.int32, (80, COLS), 0)
    spread_col = lax.broadcasted_iota(jnp.int32, (80, COLS), 1)
    spread = (spread_row == col * (COLS // TILE) + spread_col // TILE).astype(BF)
    flags = jnp.zeros((64, 80), F32)
    for q in range(2):
        pick = ((pick_col == tile_row) & ((pick_row % 16) // 8 == q)).astype(BF)
        flags = flags + jnp.dot(pick, mask_ref[q].astype(F32).astype(BF), preferred_element_type=F32)
    mexp[...] = jnp.dot(flags.astype(BF), spread, preferred_element_type=F32).reshape(4, 16, COLS)

    sends = []
    used = [0]

    def sem():
        used[0] += 1
        return used[0] - 1

    def send(src, dst, index, to):
        copy = pltpu.make_async_remote_copy(
            src_ref=src, dst_ref=dst, send_sem=send_sem.at[index], recv_sem=recv_sem.at[index],
            device_id=to, device_id_type=MESH)
        copy.start()
        sends.append(copy)

    seen = set()

    def arrived(dst, index, to):
        if index in seen:
            return
        seen.add(index)
        pltpu.make_async_remote_copy(
            src_ref=dst, dst_ref=dst, send_sem=send_sem.at[index], recv_sem=recv_sem.at[index],
            device_id=to, device_id_type=MESH).wait_recv()

    s_a = {(q, s): sem() for q in range(2) for s in range(2)}
    s_b, s_core, s_cross = ({p: sem() for p in range(PARTS)} for _ in range(3))
    s_in = {(n, p): sem() for n in range(NZ) for p in range(PARTS)}
    s_fy = {(n, p, d): sem() for n in range(2) for p in Y_FIRST for d in (1, -1, 2)}
    s_y1, s_y2 = (
        {(n, p, d): sem() for n in range(NZ) for p in range(PARTS) for d in (1, -1)} for _ in range(2))
    cuts = {n: (pl.ds(0, CUT), pl.ds(CUT, WIDE - CUT)) if n in SPLIT else (pl.ds(0, WIDE),) for n in range(NZ)}
    s_far = {(n, i, d): sem() for n in range(NZ) for i in range(len(cuts[n])) for d in (1, -1)}
    s_near = {(n, i, d, h): sem() for n in range(NZ) for i in range(len(cuts[n])) for d in (1, -1) for h in range(2)}
    lanes = [pl.ds(p * PART, PART) for p in range(PARTS)]
    parts_of = [range(q * PARTS // 2, (q + 1) * PARTS // 2) for q in range(2)]
    everything = pl.ds(0, ROWS)
    halves = {1: pl.ds(0, HALF), -1: pl.ds(HALF, HALF)}

    def partial_product(q, s):
        quarter = order[s]
        loads[q, s].wait()
        for g in range(ROWS // 32):
            flag_row = mexp[quarter, pl.ds(8 * q + g, 1), :].astype(BF)
            masked[pl.ds(32 * g, 32), :] = fbuf[q, quarter, pl.ds(32 * g, 32), :] * flag_row
        return jnp.dot(masked[...], cbuf[...], preferred_element_type=F32)

    def give_core(q, n):
        give[q, n] = partial_product(q, 2 * n).astype(BF)
        send(give.at[q, n], got_a.at[q, n], s_a[q, n], core)

    def give_pair(q):
        arrived(got_a.at[q, 0], s_a[q, 0], core)
        put_b[q] = (keep[q, 0] + got_a[q, 0].astype(F32)).astype(BF)
        for p in parts_of[q]:
            within = pl.ds((p - parts_of[q][0]) * PART, PART)
            send(put_b.at[q, everything, within], got_b.at[q, everything, within], s_b[p], pair)

    def block(n, at, p, rows=everything):
        return panels.at[layers[n], at, rows, lanes[p]]

    def finish_rows(p):
        q = p * 2 // PARTS
        within = pl.ds((p - parts_of[q][0]) * PART, PART)
        if p == parts_of[q][0]:
            arrived(got_a.at[q, 1], s_a[q, 1], core)
        arrived(got_b.at[q, everything, within], s_b[p], pair)
        rows = (keep[q, 1, :, within] + got_a[q, 1, :, within].astype(F32) + got_b[q, :, within].astype(F32)).astype(BF)
        left[pair_col, :, lanes[p]] = rows
        mine = left.at[pair_col, everything, lanes[p]]
        send(mine, block(0, y, p), s_in[0, p], pair)
        send(mine, block(0, y, p), s_in[1, p], next_chip)
        send(mine, mine, s_cross[p], core)

    load.wait()
    give_value = partial_product(0, 0).astype(BF)
    give[0, 0] = give_value
    pl.semaphore_wait(barrier, len(partners))
    send(give.at[0, 0], got_a.at[0, 0], s_a[0, 0], core)
    keep[0, 0] = partial_product(0, 1)
    give_core(1, 0)
    give_pair(0)
    keep[1, 0] = partial_product(1, 1)
    give_core(0, 1)
    give_pair(1)
    keep[0, 1] = partial_product(0, 3)
    give_core(1, 1)
    keep[1, 1] = partial_product(1, 3)

    def own_step(p):
        arrived(block(0, y, p), s_in[0, p], pair)
        send(block(0, y, p), block(0, y, p), s_in[2, p], z_near)
        left[col, :, lanes[p]] = panels[zh, y, :, lanes[p]]
        mine = left.at[col, everything, lanes[p]]
        send(mine, mine, s_core[p], core)

    def next_step(p):
        arrived(block(1, y, p), s_in[1, p], next_chip)
        send(block(1, y, p), block(1, y, p), s_in[3, p], z_far)

    def land(n, p):
        if n >= 2:
            arrived(block(n, y, p), s_in[n, p], z_far if n == 2 else z_near)

    def along_y1(n, p):
        land(n, p)
        for d in (1, -1):
            send(block(n, y, p), block(n, y, p), s_y1[n, p, d], y_dev[d])

    def along_y2(n, p):
        for d in (1, -1):
            arrived(block(n, at_y(-d), p), s_y1[n, p, d], y_dev[-d])
            part = block(n, at_y(-d), p, halves[d])
            send(part, part, s_y2[n, p, d], y_dev[d])

    def forward(n, p, steps):
        for d in steps:
            if d == 2:
                end_y2(n, p)
            whole = block(n, at_y(d), p)
            send(whole, whole, s_fy[n, p, d], z_near if n == 0 else z_far)

    def end_y2(n, p):
        for d in (1, -1):
            arrived(block(n, at_y(2), p, halves[d]), s_y2[n, p, d], y_dev[-d])

    def end_left():
        for p in range(PARTS):
            arrived(left.at[cross_col, everything, lanes[p]], s_cross[p], core)
            arrived(left.at[core_col, everything, lanes[p]], s_core[p], core)

    def ready(n, last):
        end_left()
        for p in range(PARTS):
            if n >= 2 and p in Y_FIRST:
                land(n, p)
                for d in (1, -1, 2) if last else (1, -1):
                    arrived(block(n, at_y(d), p), s_fy[n - 2, p, d], z_far if n == 2 else z_near)
            else:
                for d in (1, -1):
                    arrived(block(n, at_y(-d), p), s_y1[n, p, d], y_dev[-d])
                if last:
                    end_y2(n, p)

    def columns(n):
        return pl.ds(pl.multiple_of(layers[n] * WIDE, TILE), WIDE)

    def product(n, i=0):
        last = i == len(cuts[n]) - 1
        cut = cuts[n][i]
        ready(n, last)
        if n in SPLIT:
            slot = SPLIT.index(n)
            for at, d in ((3, 2),) if last else ((0, 0), (1, 1), (2, -1)):
                gathered[slot, pl.ds(at * ROWS, ROWS)] = panels[layers[n], at_y(d)]
            right = gathered[slot, cut]
        else:
            right = panels[layers[n]].reshape(WIDE, 2 * OCC)
        value = lax.dot_general(
            left[...].reshape(4 * ROWS, 2 * OCC), right, NT, preferred_element_type=F32)
        prod[:, :, cut] = value.reshape(4, ROWS, cut.size)
        far[n, :, cut] = prod[at_x(2), :, cut].astype(BF)
        for d in (1, -1):
            send(far.at[n, halves[d], cut], got_far.at[n, 0 if d == 1 else 1, pl.ds(0, HALF), cut], s_far[n, i, d], x_dev[d])
        for d in (1, -1):
            slot = 0 if d == 1 else 1
            mine, other = halves[d], halves[-d]
            near[n, slot, other, cut] = prod[at_x(d), other, cut].astype(BF)
            held[n, slot, :, cut] = prod[at_x(d), mine, cut]
            send(near.at[n, slot, other, cut], got_near.at[n, slot, other, cut], s_near[n, i, d, 1], x_dev[d])
        if n in SPLIT:
            turned[SPLIT.index(n), :, cut] = prod[x, :, cut]
        else:
            out_ref[:, columns(n)] = prod[x]

    def pass_on(n, i=0):
        cut = cuts[n][i]
        for d in (1, -1):
            slot = 0 if d == 1 else 1
            mine = halves[d]
            arrived(got_far.at[n, slot, pl.ds(0, HALF), cut], s_far[n, i, d], x_dev[-d])
            near[n, slot, mine, cut] = (held[n, slot, :, cut] + got_far[n, slot, :, cut].astype(F32)).astype(BF)
            send(near.at[n, slot, mine, cut], got_near.at[n, slot, mine, cut], s_near[n, i, d, 0], x_dev[d])

    def finish(n, i=0):
        cut = cuts[n][i]
        for d in (1, -1):
            slot = 0 if d == 1 else 1
            arrived(got_near.at[n, slot, halves[d], cut], s_near[n, i, d, 0], x_dev[-d])
            arrived(got_near.at[n, slot, halves[-d], cut], s_near[n, i, d, 1], x_dev[-d])
        total = got_near[n, 0, :, cut].astype(F32) + got_near[n, 1, :, cut].astype(F32)
        if n not in SPLIT:
            out_ref[:, columns(n)] += total
            return
        at = SPLIT.index(n)
        turned[at, :, cut] += total
        if i == len(cuts[n]) - 1:
            for v in range(NY):
                @pl.when(y == v)
                def _(v=v):
                    for place, d in enumerate((0, 1, -1, 2)):
                        natural[:, pl.ds((v + d) % NY * ROWS, ROWS)] = turned[at, :, pl.ds(place * ROWS, ROWS)]
            out_ref[:, columns(n)] = natural[...]

    finish_rows(0)
    finish_rows(1)
    finish_rows(2)
    next_step(0)
    along_y1(1, 0)
    finish_rows(3)
    next_step(1)
    along_y1(1, 1)
    own_step(0)
    next_step(2)
    along_y1(1, 2)
    along_y2(1, 0)
    own_step(1)
    next_step(3)
    along_y1(1, 3)
    along_y2(1, 1)
    along_y1(0, 0)
    own_step(2)
    along_y2(1, 2)
    along_y1(0, 1)
    along_y2(1, 3)
    forward(1, 3, (1, -1))
    along_y1(0, 2)
    own_step(3)
    along_y1(0, 3)
    along_y2(0, 0)
    along_y2(0, 1)
    product(1)
    forward(1, 3, (2,))
    along_y2(0, 2)
    along_y2(0, 3)
    forward(0, 3, (1, -1))
    along_y1(3, 0)
    along_y1(3, 1)
    along_y1(3, 2)
    along_y1(2, 0)
    along_y1(2, 1)
    pass_on(1)
    along_y1(2, 2)
    product(0)
    forward(0, 3, (2,))
    along_y2(3, 0)
    finish(1)
    along_y2(3, 1)
    product(3, 0)
    pass_on(0)
    along_y2(3, 2)
    along_y2(2, 0)
    along_y2(2, 1)
    pass_on(3, 0)
    along_y2(2, 2)
    product(2, 0)
    product(3, 1)
    finish(0)
    finish(3, 0)
    product(2, 1)
    pass_on(2, 0)
    pass_on(3, 1)
    pass_on(2, 1)
    finish(2, 0)
    finish(3, 1)
    finish(2, 1)
    for copy in sends:
        copy.wait_send()


def on_device(factors, orbitals, tile_mask):
    vmem = pl.BlockSpec(memory_space=pltpu.VMEM)
    hbm = pl.BlockSpec(memory_space=pl.ANY)
    return pl.pallas_call(
        kernel,
        out_shape=jax.ShapeDtypeStruct((ROWS, COLS), F32),
        in_specs=[hbm, hbm, hbm],
        out_specs=vmem,
        scratch_shapes=[
            pltpu.VMEM((2, 4, ROWS, COLS), BF),
            pltpu.VMEM((COLS, OCC), BF),
            pltpu.VMEM((2, NB // TILE, NB // TILE), jnp.int32),
            pltpu.VMEM((4, 16, COLS), F32),
            pltpu.VMEM((ROWS, COLS), BF),
            pltpu.VMEM((2, 2, ROWS, OCC), BF),
            pltpu.VMEM((2, 2, ROWS, OCC), F32),
            pltpu.VMEM((2, 2, ROWS, OCC), BF),
            pltpu.VMEM((2, ROWS, OCC), BF),
            pltpu.VMEM((2, ROWS, OCC), BF),
            pltpu.VMEM((NZ, NY, ROWS, 2 * OCC), BF),
            pltpu.VMEM((4, ROWS, 2 * OCC), BF),
            pltpu.VMEM((4, ROWS, WIDE), F32),
            pltpu.VMEM((max(1, len(SPLIT)), ROWS, WIDE), F32),
            pltpu.VMEM((ROWS, WIDE), F32),
            pltpu.VMEM((max(1, len(SPLIT)), WIDE, 2 * OCC), BF),
            pltpu.VMEM((NZ, ROWS, WIDE), BF),
            pltpu.VMEM((NZ, 2, ROWS, WIDE), BF),
            pltpu.VMEM((NZ, 2, HALF, WIDE), BF),
            pltpu.VMEM((NZ, 2, ROWS, WIDE), BF),
            pltpu.VMEM((NZ, 2, HALF, WIDE), F32),
            pltpu.SemaphoreType.DMA((10,)),
            pltpu.SemaphoreType.DMA((N_SEMS,)),
            pltpu.SemaphoreType.DMA((N_SEMS,)),
        ],
        compiler_params=pltpu.CompilerParams(
            collective_id=0, has_side_effects=True, vmem_limit_bytes=56 * 2**20),
        cost_estimate=pl.CostEstimate(flops=7 * 10**9, bytes_accessed=12 * 10**6, transcendentals=0),
        name="exchange",
    )(tile_mask, factors, orbitals)


def solution(mesh):
    placed = (P("aux", None, "row", "col"), P("col", None), P("aux", None, None))
    return jax.shard_map(
        on_device, mesh=mesh, in_specs=placed, out_specs=P(("aux", "row"), "col"), check_vma=False
    )
```

```python
import jax
import jax.numpy as jnp
from jax import lax
from jax.experimental import pallas as pl
from jax.experimental.pallas import tpu as pltpu
from jax.sharding import PartitionSpec as P

NB = 10240
TILE = 128
MESH = pl.DeviceIdType.MESH
BF = jnp.bfloat16
F32 = jnp.float32
NT = (((1,), (1,)), ((), ()))
NX, NY, NZ = 4, 4, 4
ROWS, HALF, OCC = 160, 80, 512
WIDE = NY * ROWS
COLS = NB // 4
PARTS = 4
PART = 2 * OCC // PARTS
Y_FIRST = (3,)
CUTS = ((640,), (640,), (384, 256), (384, 256))
N_SEMS = 12 + 23 * PARTS + 6 * len(Y_FIRST) + 6 * sum(map(len, CUTS))


def kernel(mask_hbm, factors_ref, orbitals_ref, out_ref,
           fbuf, cbuf, mask_ref, mexp, masked, give, keep, got_a, put_b, got_b, panels, left, prod, turned, natural, gathered,
           far, near, got_far, got_near, held, in_sem, send_sem, recv_sem):
    x = lax.axis_index("aux")
    row = lax.axis_index("row")
    col = lax.axis_index("col")
    zh, y = lax.div(row, NY), lax.rem(row, NY)
    core_col = col + 1 - 2 * lax.rem(col, 2)
    pair_col = lax.rem(col + 2, 4)
    cross_col = 3 - col

    def at_x(d):
        return lax.rem(x + d + NX, NX)

    def at_y(d):
        return lax.rem(y + d + NY, NY)

    def at_z(d):
        return lax.rem(zh + d + NZ, NZ)

    side = 2 * lax.div(col, 2) - 1
    core = {"col": core_col}
    pair = {"col": pair_col}
    next_chip = {"row": at_z(side) * NY + y, "col": pair_col}
    y_dev = {d: {"row": zh * NY + at_y(d)} for d in (1, -1)}
    z_near, z_far = {"row": at_z(side) * NY + y}, {"row": at_z(-side) * NY + y}
    x_dev = {d: {"aux": at_x(d)} for d in (1, -1)}
    layers = (zh, at_z(side), at_z(-side), at_z(2))

    barrier = pltpu.get_barrier_semaphore()
    partners = [core, pair, next_chip, y_dev[1], y_dev[-1], z_near, z_far, x_dev[1], x_dev[-1]]
    for partner in partners:
        pl.semaphore_signal(barrier, inc=1, device_id=partner, device_id_type=MESH)

    order = (core_col, col, cross_col, pair_col)
    flags_in = pltpu.make_async_copy(mask_hbm, mask_ref, in_sem.at[9])
    flags_in.start()
    loads = {}
    load = pltpu.make_async_copy(orbitals_ref, cbuf, in_sem.at[8])
    load.start()
    for n, (q, s) in enumerate(((0, 0), (0, 1), (1, 0), (1, 1), (0, 2), (0, 3), (1, 2), (1, 3))):
        piece = pltpu.make_async_copy(factors_ref.at[q, order[s]], fbuf.at[q, order[s]], in_sem.at[n])
        piece.start()
        loads[q, s] = piece

    flags_in.wait()
    pick_row = lax.broadcasted_iota(jnp.int32, (64, 80), 0)
    pick_col = lax.broadcasted_iota(jnp.int32, (64, 80), 1)
    tile_row = (pick_row // 16) * (COLS // TILE) + (row * (ROWS // 32) + pick_row % 8) // (TILE // 32)
    spread_row = lax.broadcasted_iota(jnp.int32, (80, COLS), 0)
    spread_col = lax.broadcasted_iota(jnp.int32, (80, COLS), 1)
    spread = (spread_row == col * (COLS // TILE) + spread_col // TILE).astype(BF)
    flags = jnp.zeros((64, 80), F32)
    for q in range(2):
        pick = ((pick_col == tile_row) & ((pick_row % 16) // 8 == q)).astype(BF)
        flags = flags + jnp.dot(pick, mask_ref[q].astype(F32).astype(BF), preferred_element_type=F32)
    mexp[...] = jnp.dot(flags.astype(BF), spread, preferred_element_type=F32).reshape(4, 16, COLS)

    sends = []
    used = [0]

    def sem():
        used[0] += 1
        return used[0] - 1

    def send(src, dst, index, to):
        copy = pltpu.make_async_remote_copy(
            src_ref=src, dst_ref=dst, send_sem=send_sem.at[index], recv_sem=recv_sem.at[index],
            device_id=to, device_id_type=MESH)
        copy.start()
        sends.append(copy)

    seen = set()

    def arrived(dst, index, to):
        if index in seen:
            return
        seen.add(index)
        pltpu.make_async_remote_copy(
            src_ref=dst, dst_ref=dst, send_sem=send_sem.at[index], recv_sem=recv_sem.at[index],
            device_id=to, device_id_type=MESH).wait_recv()

    s_a = {(q, s): sem() for q in range(2) for s in range(2)}
    s_b, s_core, s_cross = ({p: sem() for p in range(PARTS)} for _ in range(3))
    s_in = {(n, p): sem() for n in range(NZ) for p in range(PARTS)}
    s_fy = {(n, p, d): sem() for n in range(2) for p in Y_FIRST for d in (1, -1, 2)}
    s_y1, s_y2 = (
        {(n, p, d): sem() for n in range(NZ) for p in range(PARTS) for d in (1, -1)} for _ in range(2))
    cuts = [[pl.ds(sum(c[:i]), c[i]) for i in range(len(c))] for c in CUTS]
    s_far = {(n, i, d): sem() for n in range(NZ) for i in range(len(cuts[n])) for d in (1, -1)}
    s_near = {(n, i, d, h): sem() for n in range(NZ) for i in range(len(cuts[n])) for d in (1, -1) for h in range(2)}
    lanes = [pl.ds(p * PART, PART) for p in range(PARTS)]
    parts_of = [range(q * PARTS // 2, (q + 1) * PARTS // 2) for q in range(2)]
    everything = pl.ds(0, ROWS)
    halves = {1: pl.ds(0, HALF), -1: pl.ds(HALF, HALF)}

    def partial_product(q, s):
        quarter = order[s]
        loads[q, s].wait()
        for g in range(ROWS // 32):
            flag_row = mexp[quarter, pl.ds(8 * q + g, 1), :].astype(BF)
            masked[pl.ds(32 * g, 32), :] = fbuf[q, quarter, pl.ds(32 * g, 32), :] * flag_row
        return jnp.dot(masked[...], cbuf[...], preferred_element_type=F32)

    def give_core(q, n):
        give[q, n] = partial_product(q, 2 * n).astype(BF)
        send(give.at[q, n], got_a.at[q, n], s_a[q, n], core)

    def give_pair(q):
        arrived(got_a.at[q, 0], s_a[q, 0], core)
        put_b[q] = (keep[q, 0] + got_a[q, 0].astype(F32)).astype(BF)
        for p in parts_of[q]:
            within = pl.ds((p - parts_of[q][0]) * PART, PART)
            send(put_b.at[q, everything, within], got_b.at[q, everything, within], s_b[p], pair)

    def block(n, at, p, rows=everything):
        return panels.at[layers[n], at, rows, lanes[p]]

    def finish_rows(p):
        q = p * 2 // PARTS
        within = pl.ds((p - parts_of[q][0]) * PART, PART)
        if p == parts_of[q][0]:
            arrived(got_a.at[q, 1], s_a[q, 1], core)
        arrived(got_b.at[q, everything, within], s_b[p], pair)
        rows = (keep[q, 1, :, within] + got_a[q, 1, :, within].astype(F32) + got_b[q, :, within].astype(F32)).astype(BF)
        left[pair_col, :, lanes[p]] = rows
        mine = left.at[pair_col, everything, lanes[p]]
        send(mine, block(0, y, p), s_in[0, p], pair)
        send(mine, block(0, y, p), s_in[1, p], next_chip)
        send(mine, mine, s_cross[p], core)

    load.wait()
    give_value = partial_product(0, 0).astype(BF)
    give[0, 0] = give_value
    pl.semaphore_wait(barrier, len(partners))
    send(give.at[0, 0], got_a.at[0, 0], s_a[0, 0], core)
    keep[0, 0] = partial_product(0, 1)
    give_core(1, 0)
    give_pair(0)
    keep[1, 0] = partial_product(1, 1)
    give_core(0, 1)
    give_pair(1)
    keep[0, 1] = partial_product(0, 3)
    give_core(1, 1)
    keep[1, 1] = partial_product(1, 3)

    left_done = set()

    def own_step(p):
        left_done.add(p)
        arrived(block(0, y, p), s_in[0, p], pair)
        send(block(0, y, p), block(0, y, p), s_in[2, p], z_near)
        left[col, :, lanes[p]] = panels[zh, y, :, lanes[p]]
        mine = left.at[col, everything, lanes[p]]
        send(mine, mine, s_core[p], core)

    def next_step(p):
        arrived(block(1, y, p), s_in[1, p], next_chip)
        send(block(1, y, p), block(1, y, p), s_in[3, p], z_far)

    def land(n, p):
        if n >= 2:
            arrived(block(n, y, p), s_in[n, p], z_far if n == 2 else z_near)

    def along_y1(n, p):
        land(n, p)
        for d in (1, -1):
            send(block(n, y, p), block(n, y, p), s_y1[n, p, d], y_dev[d])

    def along_y2(n, p):
        for d in (1, -1):
            arrived(block(n, at_y(-d), p), s_y1[n, p, d], y_dev[-d])
            part = block(n, at_y(-d), p, halves[d])
            send(part, part, s_y2[n, p, d], y_dev[d])

    def forward(n, p, steps):
        for d in steps:
            if d == 2:
                end_y2(n, p)
            whole = block(n, at_y(d), p)
            send(whole, whole, s_fy[n, p, d], z_near if n == 0 else z_far)

    def end_y2(n, p):
        for d in (1, -1):
            arrived(block(n, at_y(2), p, halves[d]), s_y2[n, p, d], y_dev[-d])

    def end_left():
        for p in range(PARTS):
            arrived(left.at[cross_col, everything, lanes[p]], s_cross[p], core)
            arrived(left.at[core_col, everything, lanes[p]], s_core[p], core)

    placed = (0, 1, -1, 2)

    def blocks_of(n, i):
        first = cuts[n][i].start
        return [k for k in range(NY) if k * ROWS < first + cuts[n][i].size and (k + 1) * ROWS > first]

    placed_blocks, cuts_done = set(), set()

    def ready(n, i):
        assert len(left_done) == PARTS
        end_left()
        for k in range(NY) if len(cuts[n]) == 1 else blocks_of(n, i):
            for p in range(PARTS):
                if k == 0:
                    if n < 2:
                        arrived(block(n, y, p), s_in[n, p], pair if n == 0 else next_chip)
                    land(n, p)
                elif n >= 2 and p in Y_FIRST:
                    arrived(block(n, at_y(placed[k]), p), s_fy[n - 2, p, placed[k]], z_far if n == 2 else z_near)
                elif k == 3:
                    end_y2(n, p)
                else:
                    arrived(block(n, at_y(placed[k]), p), s_y1[n, p, -placed[k]], y_dev[placed[k]])

    def columns(n):
        return pl.ds(pl.multiple_of(layers[n] * WIDE, TILE), WIDE)

    def product(n, i=0):
        cut = cuts[n][i]
        ready(n, i)
        if len(cuts[n]) > 1:
            for k in blocks_of(n, i):
                if (n, k) in placed_blocks:
                    continue
                placed_blocks.add((n, k))
                gathered[n, pl.ds(k * ROWS, ROWS)] = panels[layers[n], at_y(placed[k])]
            right = gathered[n, cut]
        else:
            right = panels[layers[n]].reshape(WIDE, 2 * OCC)
        value = lax.dot_general(
            left[...].reshape(4 * ROWS, 2 * OCC), right, NT, preferred_element_type=F32)
        prod[:, :, cut] = value.reshape(4, ROWS, cut.size)
        far[n, :, cut] = prod[at_x(2), :, cut].astype(BF)
        for d in (1, -1):
            send(far.at[n, halves[d], cut], got_far.at[n, 0 if d == 1 else 1, pl.ds(0, HALF), cut], s_far[n, i, d], x_dev[d])
        for d in (1, -1):
            slot = 0 if d == 1 else 1
            mine, other = halves[d], halves[-d]
            near[n, slot, other, cut] = prod[at_x(d), other, cut].astype(BF)
            held[n, slot, :, cut] = prod[at_x(d), mine, cut]
            send(near.at[n, slot, other, cut], got_near.at[n, slot, other, cut], s_near[n, i, d, 1], x_dev[d])
        if len(cuts[n]) > 1:
            turned[n, :, cut] = prod[x, :, cut]
        else:
            out_ref[:, columns(n)] = prod[x]

    def pass_on(n, i=0):
        cut = cuts[n][i]
        for d in (1, -1):
            slot = 0 if d == 1 else 1
            mine = halves[d]
            arrived(got_far.at[n, slot, pl.ds(0, HALF), cut], s_far[n, i, d], x_dev[-d])
            near[n, slot, mine, cut] = (held[n, slot, :, cut] + got_far[n, slot, :, cut].astype(F32)).astype(BF)
            send(near.at[n, slot, mine, cut], got_near.at[n, slot, mine, cut], s_near[n, i, d, 0], x_dev[d])

    def finish(n, i=0):
        cut = cuts[n][i]
        for d in (1, -1):
            slot = 0 if d == 1 else 1
            arrived(got_near.at[n, slot, halves[d], cut], s_near[n, i, d, 0], x_dev[-d])
            arrived(got_near.at[n, slot, halves[-d], cut], s_near[n, i, d, 1], x_dev[-d])
        total = got_near[n, 0, :, cut].astype(F32) + got_near[n, 1, :, cut].astype(F32)
        if len(cuts[n]) == 1:
            out_ref[:, columns(n)] += total
            return
        turned[n, :, cut] += total
        cuts_done.add((n, i))
        full = [k for k in range(NY) if k in blocks_of(n, i) and all(
            (n, j) in cuts_done for j in range(len(cuts[n])) if k in blocks_of(n, j))]
        for v in range(NY):
            @pl.when(y == v)
            def _(v=v):
                for k in full:
                    natural[n, :, pl.ds((v + placed[k]) % NY * ROWS, ROWS)] = turned[n, :, pl.ds(k * ROWS, ROWS)]
        if all((n, j) in cuts_done for j in range(len(cuts[n]))):
            out_ref[:, columns(n)] = natural[n]

    finish_rows(0)
    finish_rows(1)
    finish_rows(2)
    next_step(0)
    along_y1(1, 0)
    finish_rows(3)
    next_step(1)
    along_y1(1, 1)
    next_step(2)
    along_y1(1, 2)
    own_step(0)
    next_step(3)
    along_y1(1, 3)
    along_y1(0, 0)
    along_y2(1, 0)
    own_step(1)
    along_y2(1, 1)
    along_y1(0, 1)
    along_y2(1, 2)
    own_step(2)
    along_y2(1, 3)
    along_y1(0, 2)
    forward(1, 3, (1, -1))
    own_step(3)
    along_y1(0, 3)
    along_y2(0, 0)
    along_y2(0, 1)
    product(1)
    along_y2(0, 2)
    along_y2(0, 3)
    forward(0, 3, (1, -1))
    along_y1(3, 2)
    along_y1(3, 0)
    along_y1(3, 1)
    along_y1(2, 0)
    pass_on(1)
    along_y1(2, 1)
    product(0)
    along_y2(3, 0)
    along_y1(2, 2)
    product(3, 0)
    pass_on(0)
    along_y2(3, 2)
    forward(1, 3, (2,))
    along_y2(2, 0)
    along_y2(3, 1)
    pass_on(3, 0)
    along_y2(2, 1)
    finish(1)
    forward(0, 3, (2,))
    along_y2(2, 2)
    product(2, 0)
    product(3, 1)
    product(2, 1)
    pass_on(2, 0)
    finish(3, 0)
    pass_on(3, 1)
    finish(0)
    pass_on(2, 1)
    finish(2, 0)
    finish(3, 1)
    finish(2, 1)
    for copy in sends:
        copy.wait_send()


def on_device(factors, orbitals, tile_mask):
    vmem = pl.BlockSpec(memory_space=pltpu.VMEM)
    hbm = pl.BlockSpec(memory_space=pltpu.HBM)
    return pl.pallas_call(
        kernel,
        out_shape=pltpu.VMEM((ROWS, COLS), F32),
        in_specs=[hbm, hbm, hbm],
        out_specs=vmem,
        scratch_shapes=[
            pltpu.VMEM((2, 4, ROWS, COLS), BF),
            pltpu.VMEM((COLS, OCC), BF),
            pltpu.VMEM((2, NB // TILE, NB // TILE), jnp.int32),
            pltpu.VMEM((4, 16, COLS), F32),
            pltpu.VMEM((ROWS, COLS), BF),
            pltpu.VMEM((2, 2, ROWS, OCC), BF),
            pltpu.VMEM((2, 2, ROWS, OCC), F32),
            pltpu.VMEM((2, 2, ROWS, OCC), BF),
            pltpu.VMEM((2, ROWS, OCC), BF),
            pltpu.VMEM((2, ROWS, OCC), BF),
            pltpu.VMEM((NZ, NY, ROWS, 2 * OCC), BF),
            pltpu.VMEM((4, ROWS, 2 * OCC), BF),
            pltpu.VMEM((4, ROWS, WIDE), F32),
            pltpu.VMEM((NZ, ROWS, WIDE), F32),
            pltpu.VMEM((NZ, ROWS, WIDE), F32),
            pltpu.VMEM((NZ, WIDE, 2 * OCC), BF),
            pltpu.VMEM((NZ, ROWS, WIDE), BF),
            pltpu.VMEM((NZ, 2, ROWS, WIDE), BF),
            pltpu.VMEM((NZ, 2, HALF, WIDE), BF),
            pltpu.VMEM((NZ, 2, ROWS, WIDE), BF),
            pltpu.VMEM((NZ, 2, HALF, WIDE), F32),
            pltpu.SemaphoreType.DMA((10,)),
            pltpu.SemaphoreType.DMA((N_SEMS,)),
            pltpu.SemaphoreType.DMA((N_SEMS,)),
        ],
        compiler_params=pltpu.CompilerParams(
            collective_id=0, has_side_effects=True, vmem_limit_bytes=54 * 2**20),
        cost_estimate=pl.CostEstimate(flops=7 * 10**9, bytes_accessed=12 * 10**6, transcendentals=0),
        name="exchange",
    )(pltpu.with_memory_space_constraint(tile_mask, pltpu.HBM), factors, orbitals)


def solution(mesh):
    placed = (P("aux", None, "row", "col"), P("col", None), P("aux", None, None))
    return jax.shard_map(
        on_device, mesh=mesh, in_specs=placed, out_specs=P(("aux", "row"), "col"), check_vma=False
    )
```

```python
import jax
import jax.numpy as jnp
from jax import lax
from jax.experimental import pallas as pl
from jax.experimental.pallas import tpu as pltpu
from jax.sharding import PartitionSpec as P

NB = 10240
TILE = 128
MESH = pl.DeviceIdType.MESH
BF = jnp.bfloat16
F32 = jnp.float32
NT = (((1,), (1,)), ((), ()))
NX, NY, NZ = 4, 4, 4
ROWS, HALF, OCC = 160, 80, 512
WIDE = NY * ROWS
COLS = NB // 4
PARTS = 4
PART = 2 * OCC // PARTS
Y_FIRST = (3,)
CUTS = ((640,), (640,), (384, 256), (384, 256))
N_SEMS = 12 + 23 * PARTS + 6 * len(Y_FIRST) + 6 * sum(map(len, CUTS))


def kernel(mask_hbm, factors_ref, orbitals_ref, out_ref,
           fbuf, cbuf, mask_ref, mexp, masked, give, keep, got_a, put_b, got_b, panels, left, prod, turned, natural, gathered,
           far, near, got_far, got_near, held, in_sem, send_sem, recv_sem):
    x = lax.axis_index("aux")
    row = lax.axis_index("row")
    col = lax.axis_index("col")
    zh, y = lax.div(row, NY), lax.rem(row, NY)
    core_col = col + 1 - 2 * lax.rem(col, 2)
    pair_col = lax.rem(col + 2, 4)
    cross_col = 3 - col

    def at_x(d):
        return lax.rem(x + d + NX, NX)

    def at_y(d):
        return lax.rem(y + d + NY, NY)

    def at_z(d):
        return lax.rem(zh + d + NZ, NZ)

    side = 2 * lax.div(col, 2) - 1
    core = {"col": core_col}
    pair = {"col": pair_col}
    next_chip = {"row": at_z(side) * NY + y, "col": pair_col}
    y_dev = {d: {"row": zh * NY + at_y(d)} for d in (1, -1)}
    z_near, z_far = {"row": at_z(side) * NY + y}, {"row": at_z(-side) * NY + y}
    x_dev = {d: {"aux": at_x(d)} for d in (1, -1)}
    layers = (zh, at_z(side), at_z(-side), at_z(2))

    barrier = pltpu.get_barrier_semaphore()
    partners = [core, pair, next_chip, y_dev[1], y_dev[-1], z_near, z_far, x_dev[1], x_dev[-1]]
    for partner in partners:
        pl.semaphore_signal(barrier, inc=1, device_id=partner, device_id_type=MESH)

    order = (core_col, col, cross_col, pair_col)
    flags_in = pltpu.make_async_copy(mask_hbm, mask_ref, in_sem.at[9])
    flags_in.start()
    loads = {}
    load = pltpu.make_async_copy(orbitals_ref, cbuf, in_sem.at[8])
    load.start()
    for n, (q, s) in enumerate(((0, 0), (0, 1), (1, 0), (1, 1), (0, 2), (0, 3), (1, 2), (1, 3))):
        piece = pltpu.make_async_copy(factors_ref.at[q, order[s]], fbuf.at[q, order[s]], in_sem.at[n])
        piece.start()
        loads[q, s] = piece

    flags_in.wait()
    pick_row = lax.broadcasted_iota(jnp.int32, (64, 80), 0)
    pick_col = lax.broadcasted_iota(jnp.int32, (64, 80), 1)
    tile_row = (pick_row // 16) * (COLS // TILE) + (row * (ROWS // 32) + pick_row % 8) // (TILE // 32)
    spread_row = lax.broadcasted_iota(jnp.int32, (80, COLS), 0)
    spread_col = lax.broadcasted_iota(jnp.int32, (80, COLS), 1)
    spread = (spread_row == col * (COLS // TILE) + spread_col // TILE).astype(BF)
    flags = jnp.zeros((64, 80), F32)
    for q in range(2):
        pick = ((pick_col == tile_row) & ((pick_row % 16) // 8 == q)).astype(BF)
        flags = flags + jnp.dot(pick, mask_ref[q].astype(F32).astype(BF), preferred_element_type=F32)
    mexp[...] = jnp.dot(flags.astype(BF), spread, preferred_element_type=F32).reshape(4, 16, COLS)

    sends = []
    used = [0]

    def sem():
        used[0] += 1
        return used[0] - 1

    def send(src, dst, index, to):
        copy = pltpu.make_async_remote_copy(
            src_ref=src, dst_ref=dst, send_sem=send_sem.at[index], recv_sem=recv_sem.at[index],
            device_id=to, device_id_type=MESH)
        copy.start()
        sends.append(copy)

    seen = set()

    def arrived(dst, index, to):
        if index in seen:
            return
        seen.add(index)
        pltpu.make_async_remote_copy(
            src_ref=dst, dst_ref=dst, send_sem=send_sem.at[index], recv_sem=recv_sem.at[index],
            device_id=to, device_id_type=MESH).wait_recv()

    s_a = {(q, s): sem() for q in range(2) for s in range(2)}
    s_b, s_core, s_cross = ({p: sem() for p in range(PARTS)} for _ in range(3))
    s_in = {(n, p): sem() for n in range(NZ) for p in range(PARTS)}
    s_fy = {(n, p, d): sem() for n in range(2) for p in Y_FIRST for d in (1, -1, 2)}
    s_y1, s_y2 = (
        {(n, p, d): sem() for n in range(NZ) for p in range(PARTS) for d in (1, -1)} for _ in range(2))
    cuts = [[pl.ds(sum(c[:i]), c[i]) for i in range(len(c))] for c in CUTS]
    s_far = {(n, i, d): sem() for n in range(NZ) for i in range(len(cuts[n])) for d in (1, -1)}
    s_near = {(n, i, d, h): sem() for n in range(NZ) for i in range(len(cuts[n])) for d in (1, -1) for h in range(2)}
    lanes = [pl.ds(p * PART, PART) for p in range(PARTS)]
    parts_of = [range(q * PARTS // 2, (q + 1) * PARTS // 2) for q in range(2)]
    everything = pl.ds(0, ROWS)
    halves = {1: pl.ds(0, HALF), -1: pl.ds(HALF, HALF)}

    def partial_product(q, s):
        quarter = order[s]
        loads[q, s].wait()
        for g in range(ROWS // 32):
            flag_row = mexp[quarter, pl.ds(8 * q + g, 1), :].astype(BF)
            masked[pl.ds(32 * g, 32), :] = fbuf[q, quarter, pl.ds(32 * g, 32), :] * flag_row
        return jnp.dot(masked[...], cbuf[...], preferred_element_type=F32)

    def give_core(q, n):
        give[q, n] = partial_product(q, 2 * n).astype(BF)
        send(give.at[q, n], got_a.at[q, n], s_a[q, n], core)

    def give_pair(q):
        arrived(got_a.at[q, 0], s_a[q, 0], core)
        put_b[q] = (keep[q, 0] + got_a[q, 0].astype(F32)).astype(BF)
        for p in parts_of[q]:
            within = pl.ds((p - parts_of[q][0]) * PART, PART)
            send(put_b.at[q, everything, within], got_b.at[q, everything, within], s_b[p], pair)

    def block(n, at, p, rows=everything):
        return panels.at[layers[n], at, rows, lanes[p]]

    def finish_rows(p):
        q = p * 2 // PARTS
        within = pl.ds((p - parts_of[q][0]) * PART, PART)
        if p == parts_of[q][0]:
            arrived(got_a.at[q, 1], s_a[q, 1], core)
        arrived(got_b.at[q, everything, within], s_b[p], pair)
        rows = (keep[q, 1, :, within] + got_a[q, 1, :, within].astype(F32) + got_b[q, :, within].astype(F32)).astype(BF)
        left[pair_col, :, lanes[p]] = rows
        mine = left.at[pair_col, everything, lanes[p]]
        send(mine, block(0, y, p), s_in[0, p], pair)
        send(mine, block(0, y, p), s_in[1, p], next_chip)
        send(mine, mine, s_cross[p], core)

    load.wait()
    give_value = partial_product(0, 0).astype(BF)
    give[0, 0] = give_value
    pl.semaphore_wait(barrier, len(partners))
    send(give.at[0, 0], got_a.at[0, 0], s_a[0, 0], core)
    keep[0, 0] = partial_product(0, 1)
    give_core(1, 0)
    give_pair(0)
    keep[1, 0] = partial_product(1, 1)
    give_core(0, 1)
    give_pair(1)
    keep[0, 1] = partial_product(0, 3)
    give_core(1, 1)
    keep[1, 1] = partial_product(1, 3)

    left_done = set()

    def own_step(p):
        left_done.add(p)
        arrived(block(0, y, p), s_in[0, p], pair)
        send(block(0, y, p), block(0, y, p), s_in[2, p], z_near)
        left[col, :, lanes[p]] = panels[zh, y, :, lanes[p]]
        mine = left.at[col, everything, lanes[p]]
        send(mine, mine, s_core[p], core)

    def next_step(p):
        arrived(block(1, y, p), s_in[1, p], next_chip)
        send(block(1, y, p), block(1, y, p), s_in[3, p], z_far)

    def land(n, p):
        if n >= 2:
            arrived(block(n, y, p), s_in[n, p], z_far if n == 2 else z_near)

    def along_y1(n, p):
        land(n, p)
        for d in (1, -1):
            send(block(n, y, p), block(n, y, p), s_y1[n, p, d], y_dev[d])

    def turn(n, p):
        return -1 if (p + n + n // 2) % 2 else 1

    def along_y2(n, p):
        d = turn(n, p)
        whole = block(n, at_y(-d), p)
        arrived(whole, s_y1[n, p, d], y_dev[-d])
        send(whole, whole, s_y2[n, p, d], y_dev[d])

    def end_y2(n, p):
        d = turn(n, p)
        arrived(block(n, at_y(2), p), s_y2[n, p, d], y_dev[-d])

    def forward(n, p, steps):
        for d in steps:
            whole = block(n, at_y(d), p)
            if d == 2:
                end_y2(n, p)
            else:
                arrived(whole, s_y1[n, p, -d], y_dev[d])
            send(whole, whole, s_fy[n, p, d], z_near if n == 0 else z_far)

    def end_left():
        for p in range(PARTS):
            arrived(left.at[cross_col, everything, lanes[p]], s_cross[p], core)
            arrived(left.at[core_col, everything, lanes[p]], s_core[p], core)

    placed = (0, 1, -1, 2)

    def blocks_of(n, i):
        first = cuts[n][i].start
        return [k for k in range(NY) if k * ROWS < first + cuts[n][i].size and (k + 1) * ROWS > first]

    placed_blocks, cuts_done = set(), set()

    def ready(n, i):
        assert len(left_done) == PARTS
        end_left()
        for k in range(NY) if len(cuts[n]) == 1 else blocks_of(n, i):
            for p in range(PARTS):
                if k == 0:
                    if n < 2:
                        arrived(block(n, y, p), s_in[n, p], pair if n == 0 else next_chip)
                    land(n, p)
                elif n >= 2 and p in Y_FIRST:
                    arrived(block(n, at_y(placed[k]), p), s_fy[n - 2, p, placed[k]], z_far if n == 2 else z_near)
                elif k == 3:
                    end_y2(n, p)
                else:
                    arrived(block(n, at_y(placed[k]), p), s_y1[n, p, -placed[k]], y_dev[placed[k]])

    def columns(n):
        return pl.ds(pl.multiple_of(layers[n] * WIDE, TILE), WIDE)

    def product(n, i=0):
        cut = cuts[n][i]
        ready(n, i)
        if len(cuts[n]) > 1:
            for k in blocks_of(n, i):
                if (n, k) in placed_blocks:
                    continue
                placed_blocks.add((n, k))
                gathered[n, pl.ds(k * ROWS, ROWS)] = panels[layers[n], at_y(placed[k])]
            right = gathered[n, cut]
        else:
            right = panels[layers[n]].reshape(WIDE, 2 * OCC)
        value = lax.dot_general(
            left[...].reshape(4 * ROWS, 2 * OCC), right, NT, preferred_element_type=F32)
        prod[:, :, cut] = value.reshape(4, ROWS, cut.size)
        far[n, :, cut] = prod[at_x(2), :, cut].astype(BF)
        for d in (1, -1):
            send(far.at[n, halves[d], cut], got_far.at[n, 0 if d == 1 else 1, pl.ds(0, HALF), cut], s_far[n, i, d], x_dev[d])
        for d in (1, -1):
            slot = 0 if d == 1 else 1
            mine, other = halves[d], halves[-d]
            near[n, slot, other, cut] = prod[at_x(d), other, cut].astype(BF)
            held[n, slot, :, cut] = prod[at_x(d), mine, cut]
            send(near.at[n, slot, other, cut], got_near.at[n, slot, other, cut], s_near[n, i, d, 1], x_dev[d])
        if len(cuts[n]) > 1:
            turned[n, :, cut] = prod[x, :, cut]
        else:
            out_ref[:, columns(n)] = prod[x]

    def pass_on(n, i=0):
        cut = cuts[n][i]
        for d in (1, -1):
            slot = 0 if d == 1 else 1
            mine = halves[d]
            arrived(got_far.at[n, slot, pl.ds(0, HALF), cut], s_far[n, i, d], x_dev[-d])
            near[n, slot, mine, cut] = (held[n, slot, :, cut] + got_far[n, slot, :, cut].astype(F32)).astype(BF)
            send(near.at[n, slot, mine, cut], got_near.at[n, slot, mine, cut], s_near[n, i, d, 0], x_dev[d])

    def finish(n, i=0):
        cut = cuts[n][i]
        for d in (1, -1):
            slot = 0 if d == 1 else 1
            arrived(got_near.at[n, slot, halves[d], cut], s_near[n, i, d, 0], x_dev[-d])
            arrived(got_near.at[n, slot, halves[-d], cut], s_near[n, i, d, 1], x_dev[-d])
        total = got_near[n, 0, :, cut].astype(F32) + got_near[n, 1, :, cut].astype(F32)
        if len(cuts[n]) == 1:
            out_ref[:, columns(n)] += total
            return
        turned[n, :, cut] += total
        cuts_done.add((n, i))
        full = [k for k in range(NY) if k in blocks_of(n, i) and all(
            (n, j) in cuts_done for j in range(len(cuts[n])) if k in blocks_of(n, j))]
        for v in range(NY):
            @pl.when(y == v)
            def _(v=v):
                for k in full:
                    natural[n, :, pl.ds((v + placed[k]) % NY * ROWS, ROWS)] = turned[n, :, pl.ds(k * ROWS, ROWS)]
        if all((n, j) in cuts_done for j in range(len(cuts[n]))):
            out_ref[:, columns(n)] = natural[n]

    finish_rows(0)
    finish_rows(1)
    finish_rows(2)
    next_step(0)
    along_y1(1, 0)
    finish_rows(3)
    next_step(1)
    along_y1(1, 1)
    next_step(2)
    along_y1(1, 2)
    along_y2(1, 0)
    own_step(0)
    next_step(3)
    along_y1(1, 3)
    own_step(1)
    along_y1(0, 1)
    along_y2(1, 1)
    along_y2(1, 2)
    own_step(2)
    along_y1(0, 2)
    along_y2(1, 3)
    forward(1, 3, (1, -1))
    own_step(3)
    along_y1(0, 0)
    along_y1(0, 3)
    along_y2(0, 1)
    along_y2(0, 2)
    product(1)
    along_y2(0, 0)
    along_y2(0, 3)
    along_y1(3, 0)
    along_y1(3, 2)
    along_y1(3, 1)
    forward(0, 3, (1, -1))
    along_y1(2, 0)
    pass_on(1)
    along_y1(2, 1)
    forward(1, 3, (2,))
    product(0)
    along_y1(2, 2)
    product(3, 0)
    pass_on(0)
    along_y2(3, 1)
    along_y2(3, 0)
    forward(0, 3, (2,))
    along_y2(3, 2)
    pass_on(3, 0)
    along_y2(2, 0)
    product(2, 0)
    along_y2(2, 1)
    along_y2(2, 2)
    product(3, 1)
    product(2, 1)
    pass_on(2, 0)
    pass_on(3, 1)
    pass_on(2, 1)
    finish(1)
    finish(3, 0)
    finish(2, 0)
    finish(3, 1)
    finish(0)
    finish(2, 1)
    for copy in sends:
        copy.wait_send()


def on_device(factors, orbitals, tile_mask):
    vmem = pl.BlockSpec(memory_space=pltpu.VMEM)
    hbm = pl.BlockSpec(memory_space=pltpu.HBM)
    return pl.pallas_call(
        kernel,
        out_shape=pltpu.VMEM((ROWS, COLS), F32),
        in_specs=[hbm, hbm, hbm],
        out_specs=vmem,
        scratch_shapes=[
            pltpu.VMEM((2, 4, ROWS, COLS), BF),
            pltpu.VMEM((COLS, OCC), BF),
            pltpu.VMEM((2, NB // TILE, NB // TILE), jnp.int32),
            pltpu.VMEM((4, 16, COLS), F32),
            pltpu.VMEM((ROWS, COLS), BF),
            pltpu.VMEM((2, 2, ROWS, OCC), BF),
            pltpu.VMEM((2, 2, ROWS, OCC), F32),
            pltpu.VMEM((2, 2, ROWS, OCC), BF),
            pltpu.VMEM((2, ROWS, OCC), BF),
            pltpu.VMEM((2, ROWS, OCC), BF),
            pltpu.VMEM((NZ, NY, ROWS, 2 * OCC), BF),
            pltpu.VMEM((4, ROWS, 2 * OCC), BF),
            pltpu.VMEM((4, ROWS, WIDE), F32),
            pltpu.VMEM((NZ, ROWS, WIDE), F32),
            pltpu.VMEM((NZ, ROWS, WIDE), F32),
            pltpu.VMEM((NZ, WIDE, 2 * OCC), BF),
            pltpu.VMEM((NZ, ROWS, WIDE), BF),
            pltpu.VMEM((NZ, 2, ROWS, WIDE), BF),
            pltpu.VMEM((NZ, 2, HALF, WIDE), BF),
            pltpu.VMEM((NZ, 2, ROWS, WIDE), BF),
            pltpu.VMEM((NZ, 2, HALF, WIDE), F32),
            pltpu.SemaphoreType.DMA((10,)),
            pltpu.SemaphoreType.DMA((N_SEMS,)),
            pltpu.SemaphoreType.DMA((N_SEMS,)),
        ],
        compiler_params=pltpu.CompilerParams(
            collective_id=0, has_side_effects=True, vmem_limit_bytes=54 * 2**20),
        cost_estimate=pl.CostEstimate(flops=7 * 10**9, bytes_accessed=12 * 10**6, transcendentals=0),
        name="exchange",
    )(pltpu.with_memory_space_constraint(tile_mask, pltpu.HBM), factors, orbitals)


def solution(mesh):
    placed = (P("aux", None, "row", "col"), P("col", None), P("aux", None, None))
    return jax.shard_map(
        on_device, mesh=mesh, in_specs=placed, out_specs=P(("aux", "row"), "col"), check_vma=False
    )
```

```python
import jax
import jax.numpy as jnp
from jax import lax
from jax.experimental import pallas as pl
from jax.experimental.pallas import tpu as pltpu
from jax.sharding import PartitionSpec as P

NB = 10240
TILE = 128
MESH = pl.DeviceIdType.MESH
BF = jnp.bfloat16
F32 = jnp.float32
NT = (((1,), (1,)), ((), ()))
NX, NY, NZ = 4, 4, 4
ROWS, HALF, OCC = 160, 80, 512
WIDE = NY * ROWS
COLS = NB // 4
PARTS = 4
PART = 2 * OCC // PARTS
Y_FIRST = (3,)
CUTS = ((640,), (640,), (384, 256), (384, 256))
N_SEMS = 12 + 23 * PARTS + 6 * len(Y_FIRST) + 6 * sum(map(len, CUTS))


def kernel(mask_hbm, factors_ref, orbitals_ref, out_ref,
           fbuf, cbuf, mask_ref, mexp, masked, give, keep, got_a, put_b, got_b, panels, left, prod, turned, natural, gathered,
           far, near, got_far, got_near, held, in_sem, send_sem, recv_sem):
    x = lax.axis_index("aux")
    row = lax.axis_index("row")
    col = lax.axis_index("col")
    zh, y = lax.div(row, NY), lax.rem(row, NY)
    core_col = col + 1 - 2 * lax.rem(col, 2)
    pair_col = lax.rem(col + 2, 4)
    cross_col = 3 - col

    def at_x(d):
        return lax.rem(x + d + NX, NX)

    def at_y(d):
        return lax.rem(y + d + NY, NY)

    def at_z(d):
        return lax.rem(zh + d + NZ, NZ)

    side = 2 * lax.div(col, 2) - 1
    core = {"col": core_col}
    pair = {"col": pair_col}
    next_chip = {"row": at_z(side) * NY + y, "col": pair_col}
    y_dev = {d: {"row": zh * NY + at_y(d)} for d in (1, -1)}
    z_near, z_far = {"row": at_z(side) * NY + y}, {"row": at_z(-side) * NY + y}
    x_dev = {d: {"aux": at_x(d)} for d in (1, -1)}
    layers = (zh, at_z(side), at_z(-side), at_z(2))

    barrier = pltpu.get_barrier_semaphore()
    partners = [core, pair, next_chip, y_dev[1], y_dev[-1], z_near, z_far, x_dev[1], x_dev[-1]]
    for partner in partners:
        pl.semaphore_signal(barrier, inc=1, device_id=partner, device_id_type=MESH)

    order = (core_col, col, cross_col, pair_col)
    flags_in = pltpu.make_async_copy(mask_hbm, mask_ref, in_sem.at[9])
    flags_in.start()
    loads = {}
    load = pltpu.make_async_copy(orbitals_ref, cbuf, in_sem.at[8])
    load.start()
    for n, (q, s) in enumerate(((0, 0), (0, 1), (1, 0), (1, 1), (0, 2), (0, 3), (1, 2), (1, 3))):
        piece = pltpu.make_async_copy(factors_ref.at[q, order[s]], fbuf.at[q, order[s]], in_sem.at[n])
        piece.start()
        loads[q, s] = piece

    flags_in.wait()
    pick_row = lax.broadcasted_iota(jnp.int32, (64, 80), 0)
    pick_col = lax.broadcasted_iota(jnp.int32, (64, 80), 1)
    tile_row = (pick_row // 16) * (COLS // TILE) + (row * (ROWS // 32) + pick_row % 8) // (TILE // 32)
    spread_row = lax.broadcasted_iota(jnp.int32, (80, COLS), 0)
    spread_col = lax.broadcasted_iota(jnp.int32, (80, COLS), 1)
    spread = (spread_row == col * (COLS // TILE) + spread_col // TILE).astype(BF)
    flags = jnp.zeros((64, 80), F32)
    for q in range(2):
        pick = ((pick_col == tile_row) & ((pick_row % 16) // 8 == q)).astype(BF)
        flags = flags + jnp.dot(pick, mask_ref[q].astype(F32).astype(BF), preferred_element_type=F32)
    mexp[...] = jnp.dot(flags.astype(BF), spread, preferred_element_type=F32).reshape(4, 16, COLS)

    sends = []
    used = [0]

    def sem():
        used[0] += 1
        return used[0] - 1

    def send(src, dst, index, to):
        copy = pltpu.make_async_remote_copy(
            src_ref=src, dst_ref=dst, send_sem=send_sem.at[index], recv_sem=recv_sem.at[index],
            device_id=to, device_id_type=MESH)
        copy.start()
        sends.append(copy)

    seen = set()

    def arrived(dst, index, to):
        if index in seen:
            return
        seen.add(index)
        pltpu.make_async_remote_copy(
            src_ref=dst, dst_ref=dst, send_sem=send_sem.at[index], recv_sem=recv_sem.at[index],
            device_id=to, device_id_type=MESH).wait_recv()

    s_a = {(q, s): sem() for q in range(2) for s in range(2)}
    s_b, s_core, s_cross = ({p: sem() for p in range(PARTS)} for _ in range(3))
    s_in = {(n, p): sem() for n in range(NZ) for p in range(PARTS)}
    s_fy = {(n, p, d): sem() for n in range(2) for p in Y_FIRST for d in (1, -1, 2)}
    s_y1, s_y2 = (
        {(n, p, d): sem() for n in range(NZ) for p in range(PARTS) for d in (1, -1)} for _ in range(2))
    cuts = [[pl.ds(sum(c[:i]), c[i]) for i in range(len(c))] for c in CUTS]
    s_far = {(n, i, d): sem() for n in range(NZ) for i in range(len(cuts[n])) for d in (1, -1)}
    s_near = {(n, i, d, h): sem() for n in range(NZ) for i in range(len(cuts[n])) for d in (1, -1) for h in range(2)}
    lanes = [pl.ds(p * PART, PART) for p in range(PARTS)]
    parts_of = [range(q * PARTS // 2, (q + 1) * PARTS // 2) for q in range(2)]
    everything = pl.ds(0, ROWS)
    halves = {1: pl.ds(0, HALF), -1: pl.ds(HALF, HALF)}

    def partial_product(q, s):
        quarter = order[s]
        loads[q, s].wait()
        for g in range(ROWS // 32):
            flag_row = mexp[quarter, pl.ds(8 * q + g, 1), :].astype(BF)
            masked[pl.ds(32 * g, 32), :] = fbuf[q, quarter, pl.ds(32 * g, 32), :] * flag_row
        return jnp.dot(masked[...], cbuf[...], preferred_element_type=F32)

    def give_core(q, n):
        give[q, n] = partial_product(q, 2 * n).astype(BF)
        send(give.at[q, n], got_a.at[q, n], s_a[q, n], core)

    def give_pair(q):
        arrived(got_a.at[q, 0], s_a[q, 0], core)
        put_b[q] = (keep[q, 0] + got_a[q, 0].astype(F32)).astype(BF)
        for p in parts_of[q]:
            within = pl.ds((p - parts_of[q][0]) * PART, PART)
            send(put_b.at[q, everything, within], got_b.at[q, everything, within], s_b[p], pair)

    def block(n, at, p, rows=everything):
        return panels.at[layers[n], at, rows, lanes[p]]

    def finish_rows(p):
        q = p * 2 // PARTS
        within = pl.ds((p - parts_of[q][0]) * PART, PART)
        if p == parts_of[q][0]:
            arrived(got_a.at[q, 1], s_a[q, 1], core)
        arrived(got_b.at[q, everything, within], s_b[p], pair)
        rows = (keep[q, 1, :, within] + got_a[q, 1, :, within].astype(F32) + got_b[q, :, within].astype(F32)).astype(BF)
        left[pair_col, :, lanes[p]] = rows
        mine = left.at[pair_col, everything, lanes[p]]
        send(mine, block(0, y, p), s_in[0, p], pair)
        send(mine, block(0, y, p), s_in[1, p], next_chip)
        if p == parts_of[q][-1]:
            both = left.at[pair_col, everything, pl.ds(q * OCC, OCC)]
            send(both, both, s_cross[q], core)

    load.wait()
    give_value = partial_product(0, 0).astype(BF)
    give[0, 0] = give_value
    pl.semaphore_wait(barrier, len(partners))
    send(give.at[0, 0], got_a.at[0, 0], s_a[0, 0], core)
    keep[0, 0] = partial_product(0, 1)
    give_core(1, 0)
    give_pair(0)
    keep[1, 0] = partial_product(1, 1)
    give_core(0, 1)
    give_pair(1)
    keep[0, 1] = partial_product(0, 3)
    give_core(1, 1)
    keep[1, 1] = partial_product(1, 3)

    left_done = set()

    def own_step(p):
        left_done.add(p)
        arrived(block(0, y, p), s_in[0, p], pair)
        send(block(0, y, p), block(0, y, p), s_in[2, p], z_near)
        left[col, :, lanes[p]] = panels[zh, y, :, lanes[p]]
        q = p * 2 // PARTS
        if all(other in left_done for other in parts_of[q]):
            both = left.at[col, everything, pl.ds(q * OCC, OCC)]
            send(both, both, s_core[q], core)

    def next_step(p):
        arrived(block(1, y, p), s_in[1, p], next_chip)
        send(block(1, y, p), block(1, y, p), s_in[3, p], z_far)

    def land(n, p):
        if n >= 2:
            arrived(block(n, y, p), s_in[n, p], z_far if n == 2 else z_near)

    def along_y1(n, p):
        land(n, p)
        for d in (1, -1):
            send(block(n, y, p), block(n, y, p), s_y1[n, p, d], y_dev[d])

    def turn(n, p):
        return -1 if (p + n + n // 2) % 2 else 1

    def along_y2(n, p):
        d = turn(n, p)
        whole = block(n, at_y(-d), p)
        arrived(whole, s_y1[n, p, d], y_dev[-d])
        send(whole, whole, s_y2[n, p, d], y_dev[d])

    def end_y2(n, p):
        d = turn(n, p)
        arrived(block(n, at_y(2), p), s_y2[n, p, d], y_dev[-d])

    def forward(n, p, steps):
        for d in steps:
            whole = block(n, at_y(d), p)
            if d == 2:
                end_y2(n, p)
            else:
                arrived(whole, s_y1[n, p, -d], y_dev[d])
            send(whole, whole, s_fy[n, p, d], z_near if n == 0 else z_far)

    def end_left():
        for q in range(2):
            both = pl.ds(q * OCC, OCC)
            arrived(left.at[cross_col, everything, both], s_cross[q], core)
            arrived(left.at[core_col, everything, both], s_core[q], core)

    placed = (0, 1, -1, 2)

    def blocks_of(n, i):
        first = cuts[n][i].start
        return [k for k in range(NY) if k * ROWS < first + cuts[n][i].size and (k + 1) * ROWS > first]

    placed_blocks, cuts_done = set(), set()

    def ready(n, i):
        assert len(left_done) == PARTS
        end_left()
        for k in range(NY) if len(cuts[n]) == 1 else blocks_of(n, i):
            for p in range(PARTS):
                if k == 0:
                    if n < 2:
                        arrived(block(n, y, p), s_in[n, p], pair if n == 0 else next_chip)
                    land(n, p)
                elif n >= 2 and p in Y_FIRST:
                    arrived(block(n, at_y(placed[k]), p), s_fy[n - 2, p, placed[k]], z_far if n == 2 else z_near)
                elif k == 3:
                    end_y2(n, p)
                else:
                    arrived(block(n, at_y(placed[k]), p), s_y1[n, p, -placed[k]], y_dev[placed[k]])

    def columns(n):
        return pl.ds(pl.multiple_of(layers[n] * WIDE, TILE), WIDE)

    def product(n, i=0):
        cut = cuts[n][i]
        ready(n, i)
        if len(cuts[n]) > 1:
            for k in blocks_of(n, i):
                if (n, k) in placed_blocks:
                    continue
                placed_blocks.add((n, k))
                gathered[n, pl.ds(k * ROWS, ROWS)] = panels[layers[n], at_y(placed[k])]
            right = gathered[n, cut]
        else:
            right = panels[layers[n]].reshape(WIDE, 2 * OCC)
        value = lax.dot_general(
            left[...].reshape(4 * ROWS, 2 * OCC), right, NT, preferred_element_type=F32)
        prod[:, :, cut] = value.reshape(4, ROWS, cut.size)
        far[n, :, cut] = prod[at_x(2), :, cut].astype(BF)
        for d in (1, -1):
            send(far.at[n, halves[d], cut], got_far.at[n, 0 if d == 1 else 1, pl.ds(0, HALF), cut], s_far[n, i, d], x_dev[d])
        for d in (1, -1):
            slot = 0 if d == 1 else 1
            mine, other = halves[d], halves[-d]
            near[n, slot, other, cut] = prod[at_x(d), other, cut].astype(BF)
            held[n, slot, :, cut] = prod[at_x(d), mine, cut]
            send(near.at[n, slot, other, cut], got_near.at[n, slot, other, cut], s_near[n, i, d, 1], x_dev[d])
        if len(cuts[n]) > 1:
            turned[n, :, cut] = prod[x, :, cut]
        else:
            out_ref[:, columns(n)] = prod[x]

    def pass_on(n, i=0):
        cut = cuts[n][i]
        for d in (1, -1):
            slot = 0 if d == 1 else 1
            mine = halves[d]
            arrived(got_far.at[n, slot, pl.ds(0, HALF), cut], s_far[n, i, d], x_dev[-d])
            near[n, slot, mine, cut] = (held[n, slot, :, cut] + got_far[n, slot, :, cut].astype(F32)).astype(BF)
            send(near.at[n, slot, mine, cut], got_near.at[n, slot, mine, cut], s_near[n, i, d, 0], x_dev[d])

    def finish(n, i=0):
        cut = cuts[n][i]
        for d in (1, -1):
            slot = 0 if d == 1 else 1
            arrived(got_near.at[n, slot, halves[d], cut], s_near[n, i, d, 0], x_dev[-d])
            arrived(got_near.at[n, slot, halves[-d], cut], s_near[n, i, d, 1], x_dev[-d])
        total = got_near[n, 0, :, cut].astype(F32) + got_near[n, 1, :, cut].astype(F32)
        if len(cuts[n]) == 1:
            out_ref[:, columns(n)] += total
            return
        turned[n, :, cut] += total
        cuts_done.add((n, i))
        full = [k for k in range(NY) if k in blocks_of(n, i) and all(
            (n, j) in cuts_done for j in range(len(cuts[n])) if k in blocks_of(n, j))]
        for v in range(NY):
            @pl.when(y == v)
            def _(v=v):
                for k in full:
                    natural[n, :, pl.ds((v + placed[k]) % NY * ROWS, ROWS)] = turned[n, :, pl.ds(k * ROWS, ROWS)]
        if all((n, j) in cuts_done for j in range(len(cuts[n]))):
            out_ref[:, columns(n)] = natural[n]

    finish_rows(0)
    finish_rows(1)
    finish_rows(2)
    next_step(0)
    along_y1(1, 0)
    finish_rows(3)
    next_step(1)
    along_y1(1, 1)
    next_step(2)
    along_y1(1, 2)
    along_y2(1, 0)
    own_step(0)
    next_step(3)
    along_y1(1, 3)
    own_step(1)
    along_y1(0, 1)
    along_y2(1, 1)
    along_y2(1, 2)
    own_step(2)
    along_y1(0, 2)
    along_y2(1, 3)
    forward(1, 3, (1, -1))
    own_step(3)
    along_y1(0, 0)
    along_y1(0, 3)
    along_y2(0, 1)
    along_y2(0, 2)
    product(1)
    along_y2(0, 0)
    along_y2(0, 3)
    along_y1(3, 0)
    along_y1(3, 2)
    along_y1(3, 1)
    forward(0, 3, (1, -1))
    along_y1(2, 0)
    pass_on(1)
    along_y1(2, 1)
    forward(1, 3, (2,))
    product(0)
    along_y1(2, 2)
    product(3, 0)
    pass_on(0)
    along_y2(3, 1)
    along_y2(3, 0)
    forward(0, 3, (2,))
    along_y2(3, 2)
    pass_on(3, 0)
    along_y2(2, 0)
    product(2, 0)
    along_y2(2, 1)
    along_y2(2, 2)
    product(3, 1)
    product(2, 1)
    pass_on(2, 0)
    pass_on(3, 1)
    pass_on(2, 1)
    finish(1)
    finish(3, 0)
    finish(2, 0)
    finish(3, 1)
    finish(0)
    finish(2, 1)
    for copy in sends:
        copy.wait_send()


def on_device(factors, orbitals, tile_mask):
    vmem = pl.BlockSpec(memory_space=pltpu.VMEM)
    hbm = pl.BlockSpec(memory_space=pltpu.HBM)
    return pl.pallas_call(
        kernel,
        out_shape=pltpu.VMEM((ROWS, COLS), F32),
        in_specs=[hbm, hbm, hbm],
        out_specs=vmem,
        scratch_shapes=[
            pltpu.VMEM((2, 4, ROWS, COLS), BF),
            pltpu.VMEM((COLS, OCC), BF),
            pltpu.VMEM((2, NB // TILE, NB // TILE), jnp.int32),
            pltpu.VMEM((4, 16, COLS), F32),
            pltpu.VMEM((ROWS, COLS), BF),
            pltpu.VMEM((2, 2, ROWS, OCC), BF),
            pltpu.VMEM((2, 2, ROWS, OCC), F32),
            pltpu.VMEM((2, 2, ROWS, OCC), BF),
            pltpu.VMEM((2, ROWS, OCC), BF),
            pltpu.VMEM((2, ROWS, OCC), BF),
            pltpu.VMEM((NZ, NY, ROWS, 2 * OCC), BF),
            pltpu.VMEM((4, ROWS, 2 * OCC), BF),
            pltpu.VMEM((4, ROWS, WIDE), F32),
            pltpu.VMEM((NZ, ROWS, WIDE), F32),
            pltpu.VMEM((NZ, ROWS, WIDE), F32),
            pltpu.VMEM((NZ, WIDE, 2 * OCC), BF),
            pltpu.VMEM((NZ, ROWS, WIDE), BF),
            pltpu.VMEM((NZ, 2, ROWS, WIDE), BF),
            pltpu.VMEM((NZ, 2, HALF, WIDE), BF),
            pltpu.VMEM((NZ, 2, ROWS, WIDE), BF),
            pltpu.VMEM((NZ, 2, HALF, WIDE), F32),
            pltpu.SemaphoreType.DMA((10,)),
            pltpu.SemaphoreType.DMA((N_SEMS,)),
            pltpu.SemaphoreType.DMA((N_SEMS,)),
        ],
        compiler_params=pltpu.CompilerParams(
            collective_id=0, has_side_effects=True, vmem_limit_bytes=54 * 2**20),
        cost_estimate=pl.CostEstimate(flops=7 * 10**9, bytes_accessed=12 * 10**6, transcendentals=0),
        name="exchange",
    )(pltpu.with_memory_space_constraint(tile_mask, pltpu.HBM), factors, orbitals)


def solution(mesh):
    placed = (P("aux", None, "row", "col"), P("col", None), P("aux", None, None))
    return jax.shard_map(
        on_device, mesh=mesh, in_specs=placed, out_specs=P(("aux", "row"), "col"), check_vma=False
    )
```
